256 devices in a mesh: region: 8 (over x, core), dom: 32 (over y, z).
Axes of the slice: x: 4, y: 4, z: 8, core: 2. Of those that a mesh axis runs over, the one named last changes fastest.
Arguments:
- inputs: bfloat16 [131072, 512], P(('region', 'dom')), may hold values from -6 to 6
- state_init: bfloat16 [131072, 128], P(('region', 'dom')), may hold values from -6 to 6
- neighbors: int32 [131072, 4], P(('region', 'dom')), may hold values from 0 to 575
- edge_weight: float32 [131072, 4], P(('region', 'dom')), may hold values from 0.1 to 1
- boundary: int32 [16384], P(('region', 'dom')), may hold values from 0 to 511
- w_gate: bfloat16 [3, 256, 256], replicated, may hold values from -1 to 1
- b_gate: float32 [256], replicated, may hold values from -3 to 3
- w_cand: bfloat16 [3, 256, 128], replicated, may hold values from -0.4375 to 0.4375
- b_cand: float32 [128], replicated, may hold values from -3 to 3
- w_out: bfloat16 [128, 128], replicated, may hold values from -0.5 to 0.5
- b_out: float32 [128], replicated, may hold values from -4 to 4
- inc_block: int32 [262144], P(('region', 'dom')), may hold values from 0 to 31
- inc_path: int32 [262144], P(('region', 'dom')), may hold values from 0 to 2047
- path_slot: int32 [32, 2048], P('dom'), may hold values from 0 to 2047, each once within a row
Outputs:
- state_final: bfloat16 [131072, 128], P(('region', 'dom'))
- path_times: float32 [32, 2048, 128], P('dom', 'region')
The draws below stay inside these ranges and needn't reach their ends.
Inputs may be any that keep to these rules, and one draw needn't show every extreme that they name: `path_slot`: each row is a permutation of 0 to 2047.
All inputs are finite; a program needn't handle non-finite values.
Results may differ from the reference program's by a relative error of at most 0.011.
Values may be sent and summed in bfloat16 or wider, within the bound.
A program may use at most 64 MiB of HBM per device.

```python
import math
import jax
import jax.numpy as jnp

F = 128
H = 128
P_SIZE = 128
LAGS = 4
HOPS = 2
DEG = 4
BS = 16
SEG_DEV = 512
BND = 32
NBLK_DEV = 32
ENT_DEV = 1024
PATHS_COL = 2048
SEGS = 131072
N_REGION = 8
N_DOM = 32
DEVICES = 256


def draw_neighbors(key, part):
    key = jax.random.fold_in(key, 11)
    chooser_key, local_key, remote_key = jax.random.split(key, 3)
    extent = (SEGS, DEG)
    chooser = jax.random.randint(chooser_key, extent, 0, 4, dtype=jnp.int32)
    local_rows = jax.random.randint(local_key, extent, 0, SEG_DEV, dtype=jnp.int32)
    remote_rows = jax.random.randint(remote_key, extent, SEG_DEV, SEG_DEV + 2 * BND, dtype=jnp.int32)
    picked = jnp.where(chooser < 3, remote_rows, local_rows)
    picked = picked.at[0, 0].set(0)
    return picked.at[0, DEG - 1].set(SEG_DEV + 2 * BND - 1)


def draw_w_gate(key, part):
    key = jax.random.fold_in(key, 23)
    drawn_key, strong_key = jax.random.split(key, 2)
    extent = (HOPS + 1, F + H, 2 * H)
    fan_in = (HOPS + 1) * (F + H) // 4
    drawn = jax.random.normal(drawn_key, extent, jnp.float32) * (1.0 / math.sqrt(fan_in))
    drawn = jnp.clip(drawn, -6.0 / math.sqrt(fan_in), 6.0 / math.sqrt(fan_in))
    strong_bound = 7.0 / math.sqrt(F + H)
    strong = jax.random.uniform(strong_key, extent, jnp.float32, -strong_bound, strong_bound)
    hop_index = jnp.arange(HOPS + 1, dtype=jnp.int32)[:, None, None]
    column_index = jnp.arange(2 * H, dtype=jnp.int32)[None, None, :]
    reset_mask = (hop_index == HOPS) & (column_index < H)
    return jnp.where(reset_mask, strong, drawn).astype(jnp.bfloat16)


def plant(result, rng, smallest, largest):
    longest = result.shape.index(max(result.shape))
    spots = []
    for shift in (0, 1):
        where = [jax.random.randint(jax.random.fold_in(rng, axis), (), 0, length) for axis, length in enumerate(result.shape)]
        where[longest] = (where[longest] + shift) % result.shape[longest]
        spots.append(tuple(where))
    return result.at[spots[0]].set(smallest).at[spots[1]].set(largest)


def block_scale(stream_key, shape, pieces, smallest, top_value):
    def one(axis_at, blocks):
        draws = jax.random.uniform(jax.random.fold_in(jax.random.fold_in(stream_key, 6), axis_at), (blocks,), jnp.float32, smallest / len(pieces), top_value / len(pieces))
        return jnp.repeat(jnp.exp(draws), shape[axis_at] // blocks).reshape((-1,) + (1,) * (len(shape) - axis_at - 1))

    level = one(*pieces[0])
    for cut in pieces[1:]:
        level = level * one(*cut)
    return level


def gaussian(key, shape, deviation, limit, shards=(), held_as=jnp.bfloat16):
    array = deviation * jax.random.normal(key, shape, jnp.float32)
    if shards:
        array = array * block_scale(key, shape, shards, -0.22, 0.18)
    return jnp.clip(array, -limit, limit).astype(held_as)


def setup_inputs(seed: int = 0) -> dict:
    keys = jax.random.split(jax.random.key(seed), 15)
    return {
        "inputs": gaussian(keys[0], (SEGS, LAGS * F), 1.0, 6.0, ((0, 256),)),
        "state_init": gaussian(keys[1], (SEGS, H), 1.0, 6.0, ((0, 256),)),
        "neighbors": draw_neighbors(jax.random.fold_in(keys[14], 71), 0),
        "edge_weight": jnp.clip(jnp.exp(math.log(1.0) - 2.3025851 * jax.random.uniform(keys[3], (SEGS, DEG), jnp.float32) ** block_scale(keys[3], (SEGS, DEG), ((0, 256),), -0.2, 0.2)), 0.1, 1.0),
        "boundary": plant(jax.random.randint(keys[4], (DEVICES * 2 * BND,), 0, SEG_DEV), jax.random.fold_in(keys[4], 1), 0, SEG_DEV - 1).astype(jnp.int32),
        "w_gate": draw_w_gate(jax.random.fold_in(keys[14], 71), 0),
        "b_gate": gaussian(keys[6], (2 * H,), 0.5, 3.0, (), jnp.float32),
        "w_cand": gaussian(keys[7], (HOPS + 1, F + H, H), ((HOPS + 1) * (F + H) // 4) ** -0.5, 0.4375),
        "b_cand": gaussian(keys[8], (H,), 0.5, 3.0, (), jnp.float32),
        "w_out": gaussian(keys[9], (H, P_SIZE), H ** -0.5, 0.5),
        "b_out": gaussian(keys[10], (P_SIZE,), 1.0, 4.0, (), jnp.float32),
        "inc_block": plant(jax.random.randint(keys[11], (DEVICES * ENT_DEV,), 0, NBLK_DEV), jax.random.fold_in(keys[11], 1), 0, NBLK_DEV - 1).astype(jnp.int32),
        "inc_path": plant(jax.random.randint(keys[12], (DEVICES * ENT_DEV,), 0, PATHS_COL), jax.random.fold_in(keys[12], 1), 0, PATHS_COL - 1).astype(jnp.int32),
        "path_slot": jax.vmap(lambda own: jax.random.permutation(own, PATHS_COL))(jax.random.split(keys[13], N_DOM)).reshape((N_DOM, PATHS_COL)).astype(jnp.int32),
    }


def take_rows(table, index):
    return jax.vmap(jax.vmap(lambda a, i: jnp.take(a, i, axis=0)))(table, index)


def extend(field, bnd):
    half = bnd.shape[2] // 2
    edges = take_rows(field, bnd)
    zero = jnp.zeros_like(edges[:, :1, :half])
    lower = jnp.concatenate([zero, edges[:, :-1, half:]], axis=1)
    upper = jnp.concatenate([edges[:, 1:, :half], zero], axis=1)
    return jnp.concatenate([field, lower, upper], axis=2)


def spread(field, bnd, nbr, wts):
    table = extend(field, bnd)
    acc = jnp.zeros(field.shape[:3] + (field.shape[3],), jnp.float32)
    for k in range(nbr.shape[3]):
        acc = acc + wts[..., k:k + 1] * take_rows(table, nbr[..., k]).astype(jnp.float32)
    return acc.astype(jnp.bfloat16)


def project(parts, weight, bias):
    stacked = jnp.concatenate(parts, axis=-1)
    flat = stacked.reshape(-1, stacked.shape[-1])
    wflat = weight.reshape(-1, weight.shape[-1])
    out = jnp.dot(flat, wflat, preferred_element_type=jnp.float32) + bias
    return out.reshape(stacked.shape[:3] + (weight.shape[-1],))


def reference(inputs, state_init, neighbors, edge_weight, boundary, w_gate, b_gate, w_cand, b_cand, w_out, b_out, inc_block, inc_path, path_slot):
    shape4 = (N_REGION, N_DOM, SEG_DEV)
    xall = inputs.reshape(shape4 + (LAGS * F,))
    h = state_init.reshape(shape4 + (H,)).astype(jnp.float32)
    nbr = neighbors.reshape(shape4 + (DEG,))
    wraw = edge_weight.reshape(shape4 + (DEG,))
    wts = wraw / jnp.sum(wraw, axis=-1, keepdims=True)
    bnd = boundary.reshape(N_REGION, N_DOM, 2 * BND)
    for t in range(LAGS):
        x_t = xall[..., t * F:(t + 1) * F]
        z = jnp.concatenate([x_t, h.astype(jnp.bfloat16)], axis=-1)
        s1 = spread(z, bnd, nbr, wts)
        s2 = spread(s1, bnd, nbr, wts)
        gates = project([z, s1, s2], w_gate, b_gate)
        reset = jax.nn.sigmoid(gates[..., :H])
        update = jax.nn.sigmoid(gates[..., H:])
        zc = jnp.concatenate([x_t, (reset * h).astype(jnp.bfloat16)], axis=-1)
        c1 = spread(zc, bnd, nbr, wts)
        c2 = spread(c1, bnd, nbr, wts)
        cand = jnp.tanh(project([zc, c1, c2], w_cand, b_cand))
        h = update * h + (1.0 - update) * cand
    state_final = h.astype(jnp.bfloat16)
    flat = state_final.reshape(-1, H)
    seg_time = 0.05 * jax.nn.softplus(jnp.dot(flat, w_out, preferred_element_type=jnp.float32) + b_out)
    block_time = seg_time.reshape(N_REGION * N_DOM, NBLK_DEV, BS, P_SIZE).sum(axis=2).astype(jnp.bfloat16)
    blocks = inc_block.reshape(N_REGION * N_DOM, ENT_DEV)
    vals = jax.vmap(lambda a, i: jnp.take(a, i, axis=0))(block_time, blocks).astype(jnp.float32)
    paths = inc_path.reshape(N_REGION, N_DOM, ENT_DEV)
    slots = jnp.take_along_axis(jnp.broadcast_to(path_slot[None], (N_REGION, N_DOM, PATHS_COL)), paths, axis=2)
    vals = vals.reshape(N_REGION, N_DOM, ENT_DEV, P_SIZE).transpose(1, 0, 2, 3).reshape(N_DOM, N_REGION * ENT_DEV, P_SIZE)
    slots = slots.transpose(1, 0, 2).reshape(N_DOM, N_REGION * ENT_DEV)
    path_times = jax.vmap(lambda v, i: jax.ops.segment_sum(v, i, num_segments=PATHS_COL))(vals, slots)
    return state_final.reshape(-1, H), path_times
```

```python
import functools

import jax
import jax.numpy as jnp
from jax import lax
from jax.experimental import pallas as pl
from jax.experimental.pallas import tpu as pltpu
from jax.sharding import PartitionSpec as P

MESH = pl.DeviceIdType.MESH
SEG, WIDTH, BND, NBLK, BS = 512, 128, 32, 32, 16
LAGS, ENT, PATHS = 4, 1024, 2048
SLOT_HI = PATHS // WIDTH
F32, BF16 = jnp.float32, jnp.bfloat16


def dot(a, b):
    return jnp.dot(a, b, preferred_element_type=F32)


def iota(shape, dim):
    return lax.broadcasted_iota(jnp.int32, shape, dim)


def sigmoid(v):
    return 0.5 * jnp.tanh(0.5 * v) + 0.5


def kernel(
    nr, nd,
    nbr_h, ew_h, bnd_h, h0_h, x_h, wg_h, wc_h, wo_h, bg_h, bc_h, bo_h, ib_h, ip_h, ps_h,
    sf_o, pt_o,
    nbr, ew, bnd, x, wx, wgh, wch, wo, bg, bc, bo, ib, ip, ps,
    h, hb, rhb, m, ar, pk, s, aa, g, acc, s12, sx, gx, pre, upd,
    e0, r0, ex, rx, eh, rh,
    cnt, crecv, ct, btsend, btrecv, ptv,
    load_sem, send_sem, recv_sem, c_send, c_recv, b_send, b_recv, out_sem,
):
    region, dom = lax.axis_index("region"), lax.axis_index("dom")
    up1, dn1 = lax.rem(dom + 1, nd), lax.rem(dom + nd - 1, nd)
    up2, dn2 = lax.rem(dom + 2, nd), lax.rem(dom + nd - 2, nd)
    peers = [None] + [lax.rem(region + k, nr) for k in range(1, nr)]
    own_hi = SLOT_HI // nr
    own_rows = own_hi * NBLK

    loads = []

    def load(src, dst):
        copy = pltpu.make_async_copy(src, dst, load_sem.at[len(loads)])
        copy.start()
        loads.append(copy)
        return copy

    l_graph = [load(nbr_h, nbr), load(ew_h, ew), load(bnd_h, bnd)]
    l_h0 = load(h0_h, hb)
    l_x = load(x_h, x)
    l_path = [load(ib_h, ib), load(ip_h, ip), load(ps_h, ps)]
    l_w = [
        load(wg_h.at[:, 0:WIDTH, :], wx.at[:, :, 0 : 2 * WIDTH]),
        load(wc_h.at[:, 0:WIDTH, :], wx.at[:, :, 2 * WIDTH : 3 * WIDTH]),
        load(wg_h.at[:, WIDTH : 2 * WIDTH, :], wgh),
        load(wc_h.at[:, WIDTH : 2 * WIDTH, :], wch),
        load(bg_h, bg),
        load(bc_h, bc),
        load(wo_h, wo),
        load(bo_h, bo),
    ]

    barrier = pltpu.get_barrier_semaphore()
    for there in (up1, dn1, up2, dn2):
        pl.semaphore_signal(barrier, inc=1, device_id={"dom": there}, device_id_type=MESH)
    for k in range(1, nr):
        pl.semaphore_signal(barrier, inc=1, device_id={"region": peers[k]}, device_id_type=MESH)

    for c in l_graph:
        c.wait()
    near = nbr[...]
    outside = ((dom == 0) & (near >= SEG) & (near < SEG + BND)) | (
        (dom == nd - 1) & (near >= SEG + BND)
    )
    near = jnp.where(outside, -1, near).astype(F32)
    raw = ew[...]
    wts = raw / jnp.sum(raw, axis=0, keepdims=True)
    tall = jnp.transpose(jnp.concatenate([near, wts], axis=0))
    step = 32
    lanes = iota((step, SEG + WIDTH), 1).astype(F32)
    for i in range(0, SEG, step):
        a = jnp.zeros((step, SEG + WIDTH), F32)
        for k in range(4):
            a = a + jnp.where(lanes == tall[i : i + step, k : k + 1], tall[i : i + step, 4 + k : 5 + k], 0.0)
        a = a.astype(BF16)
        m[i : i + step, 0:SEG] = a[:, 0:SEG]
        ar[i : i + step, :] = a[:, SEG:]

    turn = lax.rem(iota((2 * BND, 2 * BND), 0) + BND, 2 * BND) == iota((2 * BND, 2 * BND), 1)
    picked = jnp.sum(jnp.where(turn, bnd[...].astype(F32), 0.0), axis=1, keepdims=True)
    picker = (iota((2 * BND, SEG), 1).astype(F32) == picked).astype(F32).astype(BF16)
    pk[0 : 2 * BND, :] = picker
    pk[2 * BND :, :] = jnp.zeros((2 * BND, SEG), BF16)
    a_bnd = dot(picker, m[0:SEG, 0:SEG]).astype(BF16)
    s[0:32, :] = picker[0:32]
    s[32:64, :] = a_bnd[0:32]
    s[64:96, :] = picker[32:64]
    s[96:128, :] = a_bnd[32:64]

    sends = []

    def exchange(n, src, dst, far):
        lo, hi = far
        plan = (
            (src.at[0:64], dst.at[0:64], up1),
            (src.at[64:128], dst.at[64:128], dn1),
            (src.at[0:32, lo:hi], dst.at[128:160, lo:hi], up2),
            (src.at[64:96, lo:hi], dst.at[160:192, lo:hi], dn2),
        )
        copies = []
        for j, (a, b, there) in enumerate(plan):
            copy = pltpu.make_async_remote_copy(
                src_ref=a, dst_ref=b, send_sem=send_sem.at[n, j], recv_sem=recv_sem.at[n, j],
                device_id={"dom": there}, device_id_type=MESH,
            )
            copy.start()
            copies.append(copy)
        sends.extend(copies)
        return copies

    l_h0.wait()
    e0[:, 0:WIDTH] = dot(s[...], hb[...]).astype(BF16)
    e0[:, WIDTH:] = dot(s[...], ar[...]).astype(BF16)
    pl.semaphore_wait(barrier, 4 + nr - 1)
    first = exchange(0, e0, r0, (0, WIDTH))
    l_x.wait()
    x_moves = []
    for pair in range(2):
        cols = slice(pair * 256, pair * 256 + 256)
        ex[pair] = dot(s[...], x[:, cols]).astype(BF16)
        x_moves.append(exchange(1 + pair, ex.at[pair], rx.at[pair], (0, 256)))

    r0[192:256, :] = jnp.zeros((64, 256), BF16)
    rx[:, 192:256, :] = jnp.zeros((2, 64, 256), BF16)
    rh[:, 192:256, :] = jnp.zeros((2 * LAGS - 1, 64, WIDTH), BF16)
    row, col = iota((WIDTH, 2 * WIDTH), 0), iota((WIDTH, 2 * WIDTH), 1)
    place = ((row < 32) & (col == row)) | ((row >= 32) & (row < 64) & (col == row + 32))
    m[0:SEG, SEG:] = dot(ar[...], place.astype(F32).astype(BF16)).astype(BF16)
    aa[...] = dot(m[0:SEG, 0:SEG], m[0:SEG, :])

    for c in l_path:
        c.wait()
    path = ip[...]
    path_hi, path_lo = lax.shift_right_logical(path, 7), path & (WIDTH - 1)
    which = (iota((SLOT_HI, ENT), 0) == path_hi).astype(F32).astype(BF16)
    slots = ps[...]
    slots_hi = lax.shift_right_logical(slots, 7).astype(F32).astype(BF16)
    slots_lo = (slots & (WIDTH - 1)).astype(F32).astype(BF16)
    at_lo = iota((WIDTH, ENT), 0) == path_lo
    contract0 = (((0,), (0,)), ((), ()))
    slot_hi = jnp.sum(
        jnp.where(at_lo, lax.dot_general(slots_hi, which, contract0, preferred_element_type=F32), 0.0),
        axis=0, keepdims=True,
    )
    slot_lo = jnp.sum(
        jnp.where(at_lo, lax.dot_general(slots_lo, which, contract0, preferred_element_type=F32), 0.0),
        axis=0, keepdims=True,
    )
    target = slot_hi * NBLK + ib[...].astype(F32)
    ones_lo = (iota((WIDTH, ENT), 0).astype(F32) == slot_lo).astype(F32).astype(BF16)
    for i in range(0, SLOT_HI * NBLK, 128):
        ones = (iota((128, ENT), 0).astype(F32) + float(i) == target).astype(F32).astype(BF16)
        count = lax.dot_general(ones, ones_lo, (((1,), (1,)), ((), ())), preferred_element_type=F32)
        top = count.astype(BF16)
        cnt[0, i : i + 128, :] = top
        cnt[1, i : i + 128, :] = (count - top.astype(F32)).astype(BF16)
    c_moves = []
    for k in range(1, nr):
        copy = pltpu.make_async_remote_copy(
            src_ref=cnt.at[:, pl.ds(pl.multiple_of(peers[k] * own_rows, own_rows), own_rows), :],
            dst_ref=crecv.at[k],
            send_sem=c_send.at[k], recv_sem=c_recv.at[k],
            device_id={"region": peers[k]}, device_id_type=MESH,
        )
        copy.start()
        c_moves.append(copy)
    crecv[0] = cnt[:, pl.ds(pl.multiple_of(region * own_rows, own_rows), own_rows), :]

    for c in first:
        c.wait_recv()
    lane = iota((32, WIDTH), 1)
    b_low, b_up = r0[0:32, WIDTH:].astype(F32), r0[64:96, WIDTH:].astype(F32)
    g_row, g_col = iota((32, WIDTH), 0), iota((32, WIDTH), 1)
    g[0:32, SEG : SEG + WIDTH] = (g_col == g_row + 32).astype(F32).astype(BF16)
    g[32:64, SEG : SEG + WIDTH] = (g_col == g_row + 96).astype(F32).astype(BF16)
    g[0:32, SEG + WIDTH :] = jnp.where(lane < 32, b_low, 0.0).astype(BF16)
    g[32:64, SEG + WIDTH :] = jnp.where((lane >= 32) & (lane < 64), b_up, 0.0).astype(BF16)
    back = jnp.concatenate(
        [jnp.where((lane >= 32) & (lane < 64), b_low, 0.0), jnp.where(lane < 32, b_up, 0.0)], axis=0
    ).astype(BF16)
    g[0:64, 0:SEG] = dot(back, pk[...]).astype(BF16)
    g[64:128, :] = jnp.zeros((64, SEG + 2 * WIDTH), BF16)
    m[SEG:, :] = (aa[...] + dot(ar[...], g[...])).astype(BF16)

    for c in l_w:
        c.wait()

    def x_spread(pair):
        cols = slice(pair * 256, pair * 256 + 256)
        for c in x_moves[pair]:
            c.wait_recv()
        sx[pair] = (dot(m[:, 0:SEG], x[:, cols]) + dot(m[:, SEG:], rx[pair])).astype(BF16)

    def x_project(t):
        pair, cols = t // 2, slice((t % 2) * WIDTH, (t % 2 + 1) * WIDTH)
        bias = jnp.concatenate([bg[...], bc[...]], axis=1)
        gx[t] = (
            dot(x[:, t * WIDTH : (t + 1) * WIDTH], wx[0])
            + dot(sx[pair, 0:SEG, cols], wx[1])
            + dot(sx[pair, SEG:, cols], wx[2])
            + bias
        )

    def arrive(field, recv):
        both = acc[...] + dot(m[:, SEG:], recv)
        s12[:, 0:WIDTH] = both[0:SEG].astype(BF16)
        s12[:, WIDTH:] = both[SEG:].astype(BF16)

    def send_field(n, field):
        eh[n] = dot(s[...], field).astype(BF16)
        return exchange(3 + n, eh.at[n], rh.at[n], (0, WIDTH))

    h[...] = hb[...].astype(F32)
    x_spread(0)
    x_project(0)
    moving = None
    for t in range(LAGS):
        acc[...] = dot(m[:, 0:SEG], hb[...])
        pre[...] = gx[t, :, 0 : 2 * WIDTH] + dot(hb[...], wgh[0])
        if t == 1:
            x_project(2)
        if t == 2:
            x_project(3)
        if t == 0:
            arrive(hb, r0[:, 0:WIDTH])
        else:
            for c in moving:
                c.wait_recv()
            arrive(hb, rh[2 * t - 1])
        w12 = wgh[1:3].reshape(2 * WIDTH, 2 * WIDTH)
        reset = sigmoid(pre[:, 0:WIDTH] + dot(s12[...], w12[:, 0:WIDTH]))
        rhb[...] = (reset * h[...]).astype(BF16)
        moving = send_field(2 * t, rhb[...])
        upd[...] = sigmoid(pre[:, WIDTH:] + dot(s12[...], w12[:, WIDTH:]))
        acc[...] = dot(m[:, 0:SEG], rhb[...])
        pre[:, 0:WIDTH] = gx[t, :, 2 * WIDTH :] + dot(rhb[...], wch[0])
        if t == 0:
            x_project(1)
            x_spread(1)
        for c in moving:
            c.wait_recv()
        arrive(rhb, rh[2 * t])
        wc12 = wch[1:3].reshape(2 * WIDTH, WIDTH)
        cand = jnp.tanh(pre[:, 0:WIDTH] + dot(s12[...], wc12))
        new = cand + upd[...] * (h[...] - cand)
        h[...] = new
        hb[...] = new.astype(BF16)
        if t < LAGS - 1:
            moving = send_field(2 * t + 1, hb[...])

    out_state = pltpu.make_async_copy(hb, sf_o, out_sem.at[0])
    out_state.start()
    v = dot(hb[...], wo[...]) + bo[...]
    soft = jnp.maximum(v, 0.0) + jnp.log1p(jnp.exp(-jnp.abs(v)))
    block = 0.05 * jnp.sum(soft.reshape(NBLK, BS, WIDTH), axis=1)
    btsend[...] = block.astype(BF16)
    b_moves = []
    for k in range(1, nr):
        copy = pltpu.make_async_remote_copy(
            src_ref=btsend, dst_ref=btrecv.at[k],
            send_sem=b_send.at[k], recv_sem=b_recv.at[k],
            device_id={"region": peers[k]}, device_id_type=MESH,
        )
        copy.start()
        b_moves.append(copy)
    btrecv[0] = btsend[...]
    for c in c_moves:
        c.wait_recv()
    for plane in range(2):
        for j in range(own_hi):
            part = crecv[:, plane, j * NBLK : (j + 1) * NBLK, :].reshape(nr * NBLK, WIDTH)
            ct[plane, j * WIDTH : (j + 1) * WIDTH, :] = jnp.transpose(part)
    for c in b_moves:
        c.wait_recv()
    times = btrecv[...].reshape(nr * NBLK, WIDTH)
    ptv[...] = dot(ct[0], times) + dot(ct[1], times)
    out_path = pltpu.make_async_copy(ptv, pt_o, out_sem.at[1])
    out_path.start()
    for c in sends + c_moves + b_moves:
        c.wait_send()
    out_state.wait()
    out_path.wait()


def solution(mesh):
    nr, nd = mesh.shape["region"], mesh.shape["dom"]
    owned = PATHS // nr
    own_rows = SLOT_HI // nr * NBLK
    vmem = pltpu.VMEM
    scratch = [
        vmem((4, SEG), jnp.int32), vmem((4, SEG), F32), vmem((1, 2 * BND), jnp.int32),
        vmem((SEG, LAGS * WIDTH), BF16),
        vmem((3, WIDTH, 3 * WIDTH), BF16), vmem((3, WIDTH, 2 * WIDTH), BF16), vmem((3, WIDTH, WIDTH), BF16),
        vmem((WIDTH, WIDTH), BF16),
        vmem((1, 2 * WIDTH), F32), vmem((1, WIDTH), F32), vmem((1, WIDTH), F32),
        vmem((1, ENT), jnp.int32), vmem((1, ENT), jnp.int32), vmem((SLOT_HI, WIDTH), jnp.int32),
        vmem((SEG, WIDTH), F32), vmem((SEG, WIDTH), BF16), vmem((SEG, WIDTH), BF16),
        vmem((2 * SEG, SEG + 2 * WIDTH), BF16), vmem((SEG, WIDTH), BF16), vmem((WIDTH, SEG), BF16),
        vmem((WIDTH, SEG), BF16), vmem((SEG, SEG + 2 * WIDTH), F32), vmem((WIDTH, SEG + 2 * WIDTH), BF16),
        vmem((2 * SEG, WIDTH), F32), vmem((SEG, 2 * WIDTH), BF16), vmem((2, 2 * SEG, 2 * WIDTH), BF16),
        vmem((LAGS, SEG, 3 * WIDTH), F32), vmem((SEG, 2 * WIDTH), F32), vmem((SEG, WIDTH), F32),
        vmem((128, 256), BF16), vmem((256, 256), BF16),
        vmem((2, 128, 256), BF16), vmem((2, 256, 256), BF16),
        vmem((2 * LAGS - 1, 128, WIDTH), BF16), vmem((2 * LAGS - 1, 256, WIDTH), BF16),
        vmem((2, SLOT_HI * NBLK, WIDTH), BF16), vmem((nr, 2, own_rows, WIDTH), BF16),
        vmem((2, owned, nr * NBLK), BF16),
        vmem((NBLK, WIDTH), BF16), vmem((nr, NBLK, WIDTH), BF16), vmem((owned, WIDTH), F32),
        pltpu.SemaphoreType.DMA((16,)),
        pltpu.SemaphoreType.DMA((2 + 2 * LAGS, 4)), pltpu.SemaphoreType.DMA((2 + 2 * LAGS, 4)),
        pltpu.SemaphoreType.DMA((nr,)), pltpu.SemaphoreType.DMA((nr,)),
        pltpu.SemaphoreType.DMA((nr,)), pltpu.SemaphoreType.DMA((nr,)),
        pltpu.SemaphoreType.DMA((2,)),
    ]
    call = pl.pallas_call(
        functools.partial(kernel, nr, nd),
        out_shape=(
            jax.ShapeDtypeStruct((SEG, WIDTH), BF16),
            jax.ShapeDtypeStruct((owned, WIDTH), F32),
        ),
        in_specs=[pl.BlockSpec(memory_space=pl.ANY)] * 14,
        out_specs=(pl.BlockSpec(memory_space=pl.ANY), pl.BlockSpec(memory_space=pl.ANY)),
        scratch_shapes=scratch,
        compiler_params=pltpu.CompilerParams(
            collective_id=0, has_side_effects=True, vmem_limit_bytes=40 * 1024 * 1024
        ),
        cost_estimate=pl.CostEstimate(flops=6 * 10**9, bytes_accessed=2 * 10**6, transcendentals=10**6),
    )

    def per_device(
        inputs, state_init, neighbors, edge_weight, boundary, w_gate, b_gate, w_cand, b_cand,
        w_out, b_out, inc_block, inc_path, path_slot,
    ):
        state, paths = call(
            jnp.transpose(neighbors), jnp.transpose(edge_weight), boundary.reshape(1, -1),
            state_init, inputs, w_gate, w_cand, w_out,
            b_gate.reshape(1, -1), b_cand.reshape(1, -1), b_out.reshape(1, -1),
            inc_block.reshape(1, -1), inc_path.reshape(1, -1), path_slot.reshape(SLOT_HI, WIDTH),
        )
        return state, paths[None]

    both = ("region", "dom")
    placed = (
        P(both, None), P(both, None), P(both, None), P(both, None), P(both),
        P(), P(), P(), P(), P(), P(), P(both), P(both), P("dom", None),
    )
    return jax.shard_map(
        per_device,
        mesh=mesh,
        in_specs=placed,
        out_specs=(P(both, None), P("dom", "region", None)),
        check_vma=False,
    )
```

```python
import functools

import jax
import jax.numpy as jnp
from jax import lax
from jax.experimental import pallas as pl
from jax.experimental.pallas import tpu as pltpu
from jax.sharding import PartitionSpec as P

MESH = pl.DeviceIdType.MESH
SEG, WIDTH, BND, NBLK, BS = 512, 128, 32, 32, 16
LAGS, ENT, PATHS = 4, 1024, 2048
SLOT_HI = PATHS // WIDTH
F32, BF16 = jnp.float32, jnp.bfloat16


def dot(a, b):
    return jnp.dot(a, b, preferred_element_type=F32)


def iota(shape, dim):
    return lax.broadcasted_iota(jnp.int32, shape, dim)


def sigmoid(v):
    return 0.5 * jnp.tanh(0.5 * v) + 0.5


def kernel(
    nr, nd,
    nbr_h, ew_h, bnd_h, h0_h, x_h, wg_h, wc_h, wo_h, bg_h, bc_h, bo_h, ib_h, ip_h, ps_h,
    sf_o, pt_o,
    nbr, ew, bnd, x, wx, wgh, wch, wo, bg, bc, bo, ib, ip, ps,
    h, hb, rhb, m, ar, pk, s, aa, g, acc, s12, sx, gx, pre, upd,
    e0, r0, ex, rx, eh, rh,
    cnt, crecv, ct, btsend, btrecv,
    load_sem, send_sem, recv_sem, c_send, c_recv, b_send, b_recv,
):
    region, dom = lax.axis_index("region"), lax.axis_index("dom")
    hops = (1, -1, 2, -2)
    valid = [dom + hop < nd if hop > 0 else dom + hop >= 0 for hop in hops]
    source = [valid[1], valid[0], valid[3], valid[2]]
    guests = sum(v.astype(jnp.int32) for v in valid)

    def to_each(act):
        for j in (2, 3, 0, 1):
            pl.when(valid[j])(functools.partial(act, j, {"dom": dom + hops[j]}))

    peers = [None] + [lax.rem(region + k, nr) for k in range(1, nr)]
    own_hi = SLOT_HI // nr
    own_rows = own_hi * NBLK

    loads = []

    def load(src, dst):
        copy = pltpu.make_async_copy(src, dst, load_sem.at[len(loads)])
        copy.start()
        loads.append(copy)
        return copy

    l_graph = [load(nbr_h, nbr.at[0:4]), load(ew_h, ew.at[0:4]), load(bnd_h, bnd)]
    l_h0 = load(h0_h, hb)
    l_x = load(x_h, x)
    l_path = [load(ib_h, ib), load(ip_h, ip), load(ps_h, ps)]
    l_w = [
        load(wg_h.at[:, 0:WIDTH, :], wx.at[:, :, 0 : 2 * WIDTH]),
        load(wc_h.at[:, 0:WIDTH, :], wx.at[:, :, 2 * WIDTH : 3 * WIDTH]),
        load(wg_h.at[:, WIDTH : 2 * WIDTH, :], wgh),
        load(wc_h.at[:, WIDTH : 2 * WIDTH, :], wch),
        load(bg_h, bg),
        load(bc_h, bc),
        load(wo_h, wo),
        load(bo_h, bo),
    ]

    r0[192:256, :] = jnp.zeros((64, 256), BF16)
    rx[:, 192:256, :] = jnp.zeros((2, 64, 256), BF16)
    rh[:, 192:256, :] = jnp.zeros((2 * LAGS - 1, 64, WIDTH), BF16)

    @pl.when((dom < 2) | (dom >= nd - 2))
    def _():
        r0[0:192, :] = jnp.zeros((192, 256), BF16)
        rx[:, 0:192, :] = jnp.zeros((2, 192, 256), BF16)
        rh[:, 0:192, :] = jnp.zeros((2 * LAGS - 1, 192, WIDTH), BF16)

    barrier = pltpu.get_barrier_semaphore()
    to_each(lambda j, there: pl.semaphore_signal(barrier, inc=1, device_id=there, device_id_type=MESH))
    for k in range(1, nr):
        pl.semaphore_signal(barrier, inc=1, device_id={"region": peers[k]}, device_id_type=MESH)

    for c in l_graph:
        c.wait()
    near = nbr[...]
    outside = ((dom == 0) & (near >= SEG) & (near < SEG + BND)) | (
        (dom == nd - 1) & (near >= SEG + BND)
    )
    near = jnp.where(outside, -1, near).astype(F32)
    wts = ew[...] / (ew[0:1, :] + ew[1:2, :] + ew[2:3, :] + ew[3:4, :])
    rows, tall = jnp.transpose(near), jnp.transpose(wts)
    step = 32
    lanes = iota((step, SEG + WIDTH), 1).astype(F32)
    for i in range(0, SEG, step):
        a = jnp.zeros((step, SEG + WIDTH), F32)
        for k in range(4):
            a = a + jnp.where(lanes == rows[i : i + step, k : k + 1], tall[i : i + step, k : k + 1], 0.0)
        a = a.astype(BF16)
        m[i : i + step, 0:SEG] = a[:, 0:SEG]
        ar[i : i + step, :] = a[:, SEG:]

    turn = lax.rem(iota((2 * BND, 2 * BND), 0) + BND, 2 * BND) == iota((2 * BND, 2 * BND), 1)
    picked = jnp.sum(jnp.where(turn, bnd[...].astype(F32), 0.0), axis=1, keepdims=True)
    picker = (iota((2 * BND, SEG), 1).astype(F32) == picked).astype(F32).astype(BF16)
    pk[0 : 2 * BND, :] = picker
    pk[2 * BND :, :] = jnp.zeros((2 * BND, SEG), BF16)
    a_bnd = dot(picker, m[0:SEG, 0:SEG]).astype(BF16)
    s[0:32, :] = picker[0:32]
    s[32:64, :] = a_bnd[0:32]
    s[64:96, :] = picker[32:64]
    s[96:128, :] = a_bnd[32:64]

    sends = []

    def exchange(n, src, dst, width, far_width):
        def move(j, there):
            first, size = (0, 64)[j % 2], (64, 32)[j // 2]
            base = (0, 64, 128, 160)[j]
            cols = slice(0, far_width if j >= 2 else width)
            return pltpu.make_async_remote_copy(
                src_ref=src.at[first : first + size, cols], dst_ref=dst.at[base : base + size, cols],
                send_sem=send_sem.at[n, j], recv_sem=recv_sem.at[n, j],
                device_id=there, device_id_type=MESH,
            )

        to_each(lambda j, there: move(j, there).start())
        moves = [move(j, {"dom": lax.rem(dom + 1, nd)}) for j in range(4)]
        sends.extend(enumerate(moves))
        return moves

    def received(moves, which):
        for j in which:
            pl.when(source[j])(moves[j].wait_recv)

    l_h0.wait()
    e0[:, 0:WIDTH] = dot(s[...], hb[...]).astype(BF16)
    e0[:, WIDTH:] = dot(s[...], ar[...]).astype(BF16)
    pl.semaphore_wait(barrier, guests + nr - 1)
    first = exchange(0, e0, r0, 256, WIDTH)
    l_x.wait()
    x_moves = []
    for pair in range(2):
        cols = slice(pair * 256, pair * 256 + 256)
        ex[pair] = dot(s[...], x[:, cols]).astype(BF16)
        x_moves.append(exchange(1 + pair, ex.at[pair], rx.at[pair], 256, 256))

    row, col = iota((WIDTH, 2 * WIDTH), 0), iota((WIDTH, 2 * WIDTH), 1)
    place = ((row < 32) & (col == row)) | ((row >= 32) & (row < 64) & (col == row + 32))
    m[0:SEG, SEG:] = dot(ar[...], place.astype(F32).astype(BF16)).astype(BF16)
    aa[...] = dot(m[0:SEG, 0:SEG], m[0:SEG, :])

    for c in l_path:
        c.wait()
    path = ip[...]
    path_hi, path_lo = lax.shift_right_logical(path, 7), path & (WIDTH - 1)
    which = (iota((SLOT_HI, ENT), 0) == path_hi).astype(F32).astype(BF16)
    slots = ps[...]
    slots_hi = lax.shift_right_logical(slots, 7).astype(F32).astype(BF16)
    slots_lo = (slots & (WIDTH - 1)).astype(F32).astype(BF16)
    at_lo = iota((WIDTH, ENT), 0) == path_lo
    contract0 = (((0,), (0,)), ((), ()))
    slot_hi = jnp.sum(
        jnp.where(at_lo, lax.dot_general(slots_hi, which, contract0, preferred_element_type=F32), 0.0),
        axis=0, keepdims=True,
    )
    slot_lo = jnp.sum(
        jnp.where(at_lo, lax.dot_general(slots_lo, which, contract0, preferred_element_type=F32), 0.0),
        axis=0, keepdims=True,
    )
    target = slot_hi * NBLK + ib[...].astype(F32)
    ones_lo = (iota((WIDTH, ENT), 0).astype(F32) == slot_lo).astype(F32).astype(BF16)
    for i in range(0, SLOT_HI * NBLK, 128):
        ones = (iota((128, ENT), 0).astype(F32) + float(i) == target).astype(F32).astype(BF16)
        count = lax.dot_general(ones, ones_lo, (((1,), (1,)), ((), ())), preferred_element_type=F32)
        top = count.astype(BF16)
        cnt[0, i : i + 128, :] = top
        cnt[1, i : i + 128, :] = (count - top.astype(F32)).astype(BF16)
    c_moves = []
    for k in range(1, nr):
        copy = pltpu.make_async_remote_copy(
            src_ref=cnt.at[:, pl.ds(pl.multiple_of(peers[k] * own_rows, own_rows), own_rows), :],
            dst_ref=crecv.at[k],
            send_sem=c_send.at[k], recv_sem=c_recv.at[k],
            device_id={"region": peers[k]}, device_id_type=MESH,
        )
        copy.start()
        c_moves.append(copy)
    crecv[0] = cnt[:, pl.ds(pl.multiple_of(region * own_rows, own_rows), own_rows), :]

    received(first, range(4))
    lane = iota((32, WIDTH), 1)
    b_low, b_up = r0[0:32, WIDTH:].astype(F32), r0[64:96, WIDTH:].astype(F32)
    g_row, g_col = iota((32, WIDTH), 0), iota((32, WIDTH), 1)
    g[0:32, SEG : SEG + WIDTH] = (g_col == g_row + 32).astype(F32).astype(BF16)
    g[32:64, SEG : SEG + WIDTH] = (g_col == g_row + 96).astype(F32).astype(BF16)
    g[0:32, SEG + WIDTH :] = jnp.where(lane < 32, b_low, 0.0).astype(BF16)
    g[32:64, SEG + WIDTH :] = jnp.where((lane >= 32) & (lane < 64), b_up, 0.0).astype(BF16)
    back = jnp.concatenate(
        [jnp.where((lane >= 32) & (lane < 64), b_low, 0.0), jnp.where(lane < 32, b_up, 0.0)], axis=0
    ).astype(BF16)
    g[0:64, 0:SEG] = dot(back, pk[...]).astype(BF16)
    g[64:128, :] = jnp.zeros((64, SEG + 2 * WIDTH), BF16)
    m[SEG:, :] = (aa[...] + dot(ar[...], g[...])).astype(BF16)

    for c in l_w:
        c.wait()

    def x_spread(pair):
        cols = slice(pair * 256, pair * 256 + 256)
        received(x_moves[pair], range(4))
        sx[pair] = (dot(m[:, 0:SEG], x[:, cols]) + dot(m[:, SEG:], rx[pair])).astype(BF16)

    def x_project(t):
        pair, cols = t // 2, slice((t % 2) * WIDTH, (t % 2 + 1) * WIDTH)
        bias = jnp.concatenate([bg[...], bc[...]], axis=1)
        gx[t] = (
            dot(x[:, t * WIDTH : (t + 1) * WIDTH], wx[0])
            + dot(sx[pair, 0:SEG, cols], wx[1])
            + dot(sx[pair, SEG:, cols], wx[2])
            + bias
        )

    def arrive(moves, recv):
        if moves is not None:
            received(moves, (0, 1))
        near = acc[...] + dot(m[:, SEG : SEG + WIDTH], recv[0:128])
        s12[:, 0:WIDTH] = near[0:SEG].astype(BF16)
        if moves is not None:
            received(moves, (2, 3))
        far = near[SEG:] + dot(m[SEG:, SEG + WIDTH :], recv[128:256])
        s12[:, WIDTH:] = far.astype(BF16)

    def send_field(n, field):
        eh[n] = dot(s[...], field).astype(BF16)
        return exchange(3 + n, eh.at[n], rh.at[n], WIDTH, WIDTH)

    h[...] = hb[...].astype(F32)
    x_spread(0)
    x_project(0)
    moving = None
    for t in range(LAGS):
        acc[...] = dot(m[:, 0:SEG], hb[...])
        pre[...] = gx[t, :, 0 : 2 * WIDTH] + dot(hb[...], wgh[0])
        if t == 1:
            x_project(2)
        if t == 2:
            x_project(3)
        if t == 0:
            arrive(None, r0.at[:, 0:WIDTH])
        else:
            arrive(moving, rh.at[2 * t - 1])
        w12 = wgh[1:3].reshape(2 * WIDTH, 2 * WIDTH)
        reset = sigmoid(pre[:, 0:WIDTH] + dot(s12[...], w12[:, 0:WIDTH]))
        rhb[...] = (reset * h[...]).astype(BF16)
        moving = send_field(2 * t, rhb[...])
        upd[...] = sigmoid(pre[:, WIDTH:] + dot(s12[...], w12[:, WIDTH:]))
        acc[...] = dot(m[:, 0:SEG], rhb[...])
        pre[:, 0:WIDTH] = gx[t, :, 2 * WIDTH :] + dot(rhb[...], wch[0])
        if t == 0:
            x_project(1)
            x_spread(1)
        arrive(moving, rh.at[2 * t])
        wc12 = wch[1:3].reshape(2 * WIDTH, WIDTH)
        cand = jnp.tanh(pre[:, 0:WIDTH] + dot(s12[...], wc12))
        new = cand + upd[...] * (h[...] - cand)
        h[...] = new
        (hb if t < LAGS - 1 else sf_o)[...] = new.astype(BF16)
        if t < LAGS - 1:
            moving = send_field(2 * t + 1, hb[...])

    v = dot(sf_o[...], wo[...]) + bo[...]
    soft = jnp.maximum(v, 0.0) + jnp.log1p(jnp.exp(-jnp.abs(v)))
    block = 0.05 * jnp.sum(soft.reshape(NBLK, BS, WIDTH), axis=1)
    btsend[...] = block.astype(BF16)
    b_moves = []
    for k in range(1, nr):
        copy = pltpu.make_async_remote_copy(
            src_ref=btsend, dst_ref=btrecv.at[k],
            send_sem=b_send.at[k], recv_sem=b_recv.at[k],
            device_id={"region": peers[k]}, device_id_type=MESH,
        )
        copy.start()
        b_moves.append(copy)
    btrecv[0] = btsend[...]
    for c in c_moves:
        c.wait_recv()
    for plane in range(2):
        for j in range(own_hi):
            part = crecv[:, plane, j * NBLK : (j + 1) * NBLK, :].reshape(nr * NBLK, WIDTH)
            ct[plane, j * WIDTH : (j + 1) * WIDTH, :] = jnp.transpose(part)
    for c in b_moves:
        c.wait_recv()
    times = btrecv[...].reshape(nr * NBLK, WIDTH)
    pt_o[...] = dot(ct[0], times) + dot(ct[1], times)
    for j, c in sends:
        pl.when(valid[j])(c.wait_send)
    for c in c_moves + b_moves:
        c.wait_send()


def solution(mesh):
    nr, nd = mesh.shape["region"], mesh.shape["dom"]
    owned = PATHS // nr
    own_rows = SLOT_HI // nr * NBLK
    vmem = pltpu.VMEM
    scratch = [
        vmem((8, SEG), jnp.int32), vmem((8, SEG), F32), vmem((1, 2 * BND), jnp.int32),
        vmem((SEG, LAGS * WIDTH), BF16),
        vmem((3, WIDTH, 3 * WIDTH), BF16), vmem((3, WIDTH, 2 * WIDTH), BF16), vmem((3, WIDTH, WIDTH), BF16),
        vmem((WIDTH, WIDTH), BF16),
        vmem((1, 2 * WIDTH), F32), vmem((1, WIDTH), F32), vmem((1, WIDTH), F32),
        vmem((1, ENT), jnp.int32), vmem((1, ENT), jnp.int32), vmem((SLOT_HI, WIDTH), jnp.int32),
        vmem((SEG, WIDTH), F32), vmem((SEG, WIDTH), BF16), vmem((SEG, WIDTH), BF16),
        vmem((2 * SEG, SEG + 2 * WIDTH), BF16), vmem((SEG, WIDTH), BF16), vmem((WIDTH, SEG), BF16),
        vmem((WIDTH, SEG), BF16), vmem((SEG, SEG + 2 * WIDTH), F32), vmem((WIDTH, SEG + 2 * WIDTH), BF16),
        vmem((2 * SEG, WIDTH), F32), vmem((SEG, 2 * WIDTH), BF16), vmem((2, 2 * SEG, 2 * WIDTH), BF16),
        vmem((LAGS, SEG, 3 * WIDTH), F32), vmem((SEG, 2 * WIDTH), F32), vmem((SEG, WIDTH), F32),
        vmem((128, 256), BF16), vmem((256, 256), BF16),
        vmem((2, 128, 256), BF16), vmem((2, 256, 256), BF16),
        vmem((2 * LAGS - 1, 128, WIDTH), BF16), vmem((2 * LAGS - 1, 256, WIDTH), BF16),
        vmem((2, SLOT_HI * NBLK, WIDTH), BF16), vmem((nr, 2, own_rows, WIDTH), BF16),
        vmem((2, owned, nr * NBLK), BF16),
        vmem((NBLK, WIDTH), BF16), vmem((nr, NBLK, WIDTH), BF16),
        pltpu.SemaphoreType.DMA((16,)),
        pltpu.SemaphoreType.DMA((2 + 2 * LAGS, 4)), pltpu.SemaphoreType.DMA((2 + 2 * LAGS, 4)),
        pltpu.SemaphoreType.DMA((nr,)), pltpu.SemaphoreType.DMA((nr,)),
        pltpu.SemaphoreType.DMA((nr,)), pltpu.SemaphoreType.DMA((nr,)),
    ]
    call = pl.pallas_call(
        functools.partial(kernel, nr, nd),
        out_shape=(
            vmem((SEG, WIDTH), BF16),
            vmem((owned, WIDTH), F32),
        ),
        in_specs=[pl.BlockSpec(memory_space=pl.ANY)] * 14,
        out_specs=(pl.BlockSpec(memory_space=pltpu.VMEM), pl.BlockSpec(memory_space=pltpu.VMEM)),
        scratch_shapes=scratch,
        compiler_params=pltpu.CompilerParams(
            collective_id=0, has_side_effects=True, vmem_limit_bytes=56 * 1024 * 1024
        ),
        cost_estimate=pl.CostEstimate(flops=6 * 10**9, bytes_accessed=2 * 10**6, transcendentals=10**6),
    )

    def per_device(
        inputs, state_init, neighbors, edge_weight, boundary, w_gate, b_gate, w_cand, b_cand,
        w_out, b_out, inc_block, inc_path, path_slot,
    ):
        state, paths = call(
            jnp.transpose(neighbors), jnp.transpose(edge_weight), boundary.reshape(1, -1),
            state_init, inputs, w_gate, w_cand, w_out,
            b_gate.reshape(1, -1), b_cand.reshape(1, -1), b_out.reshape(1, -1),
            inc_block.reshape(1, -1), inc_path.reshape(1, -1), path_slot.reshape(SLOT_HI, WIDTH),
        )
        return state, paths[None]

    both = ("region", "dom")
    placed = (
        P(both, None), P(both, None), P(both, None), P(both, None), P(both),
        P(), P(), P(), P(), P(), P(), P(both), P(both), P("dom", None),
    )
    return jax.shard_map(
        per_device,
        mesh=mesh,
        in_specs=placed,
        out_specs=(P(both, None), P("dom", "region", None)),
        check_vma=False,
    )
```

```python
import functools

import jax
import jax.numpy as jnp
from jax import lax
from jax.experimental import pallas as pl
from jax.experimental.pallas import tpu as pltpu
from jax.sharding import PartitionSpec as P

MESH = pl.DeviceIdType.MESH
SEG, WIDTH, BND, NBLK, BS = 512, 128, 32, 32, 16
LAGS, ENT, PATHS = 4, 1024, 2048
SLOT_HI = PATHS // WIDTH
F32, BF16 = jnp.float32, jnp.bfloat16


def dot(a, b):
    return jnp.dot(a, b, preferred_element_type=F32)


def iota(shape, dim):
    return lax.broadcasted_iota(jnp.int32, shape, dim)


def sigmoid(v):
    return 0.5 * jnp.tanh(0.5 * v) + 0.5


def kernel(
    nr, nd,
    nbr_h, ew_h, bnd_h, h0_h, x_h, wg_h, wc_h, wo_h, bg_h, bc_h, bo_h, ib_h, ip_h, ps_h,
    sf_o, pt_o,
    nbr, ew, bnd, x, wx, wgh, wch, wo, bg, bc, bo, ib, ip, ps,
    h, hb, rhb, m, ar, pk, s, aa, g, s12, sx, gx, pre, upd,
    e0, r0, ex, rx, eh, rh,
    cnt, crecv, ct, btsend, btrecv,
    load_sem, send_sem, recv_sem, c_send, c_recv, b_send, b_recv,
):
    region, dom = lax.axis_index("region"), lax.axis_index("dom")
    hops = (1, -1, 2, -2)
    valid = [dom + hop < nd if hop > 0 else dom + hop >= 0 for hop in hops]
    source = [valid[1], valid[0], valid[3], valid[2]]
    guests = sum(v.astype(jnp.int32) for v in valid)

    def to_each(act):
        for j in (2, 3, 0, 1):
            pl.when(valid[j])(functools.partial(act, j, {"dom": dom + hops[j]}))

    peers = [None] + [lax.rem(region + k, nr) for k in range(1, nr)]
    own_hi = SLOT_HI // nr
    own_rows = own_hi * NBLK

    loads = []

    def load(src, dst):
        copy = pltpu.make_async_copy(src, dst, load_sem.at[len(loads)])
        copy.start()
        loads.append(copy)
        return copy

    l_graph = [load(nbr_h, nbr.at[0:4]), load(ew_h, ew.at[0:4]), load(bnd_h, bnd)]
    l_h0 = load(h0_h, hb)
    l_x = load(x_h, x)
    l_path = [load(ib_h, ib), load(ip_h, ip), load(ps_h, ps)]
    l_w = [
        load(wg_h.at[:, 0:WIDTH, :], wx.at[:, :, 0 : 2 * WIDTH]),
        load(wc_h.at[:, 0:WIDTH, :], wx.at[:, :, 2 * WIDTH : 3 * WIDTH]),
        load(wg_h.at[:, WIDTH : 2 * WIDTH, :], wgh),
        load(wc_h.at[:, WIDTH : 2 * WIDTH, :], wch),
        load(bg_h, bg),
        load(bc_h, bc),
        load(wo_h, wo),
        load(bo_h, bo),
    ]

    r0[192:256, :] = jnp.zeros((64, 3 * WIDTH), BF16)
    rx[:, 192:256, :] = jnp.zeros((2, 64, 256), BF16)

    @pl.when((dom < 2) | (dom >= nd - 2))
    def _():
        r0[0:192, :] = jnp.zeros((192, 3 * WIDTH), BF16)
        rx[:, 0:192, :] = jnp.zeros((2, 192, 256), BF16)
        rh[...] = jnp.zeros((2 * LAGS - 1, 192, WIDTH), BF16)

    barrier = pltpu.get_barrier_semaphore()
    to_each(lambda j, there: pl.semaphore_signal(barrier, inc=1, device_id=there, device_id_type=MESH))
    for k in range(1, nr):
        pl.semaphore_signal(barrier, inc=1, device_id={"region": peers[k]}, device_id_type=MESH)

    for c in l_graph:
        c.wait()
    near = nbr[...]
    outside = ((dom == 0) & (near >= SEG) & (near < SEG + BND)) | (
        (dom == nd - 1) & (near >= SEG + BND)
    )
    near = jnp.where(outside, -1, near)
    wts = ew[...] / (ew[0:1, :] + ew[1:2, :] + ew[2:3, :] + ew[3:4, :])
    turn = lax.rem(iota((2 * BND, 2 * BND), 0) + BND, 2 * BND) == iota((2 * BND, 2 * BND), 1)
    picked = jnp.sum(jnp.where(turn, bnd[...].astype(F32), 0.0), axis=1, keepdims=True)
    picker = (iota((2 * BND, SEG), 1).astype(F32) == picked).astype(F32).astype(BF16)
    pk[0 : 2 * BND, :] = picker
    pk[2 * BND :, :] = jnp.zeros((2 * BND, SEG), BF16)
    w_top = wts.astype(BF16).astype(F32)
    edges = jnp.concatenate(
        [lax.shift_right_arithmetic(near, 3).astype(F32), (near & 7).astype(F32), w_top, wts - w_top], axis=0
    ).astype(BF16)
    chosen = lax.dot_general(picker, edges, (((1,), (1,)), ((), ())), preferred_element_type=F32)
    at = iota((2 * BND, SEG + WIDTH), 1).astype(F32)
    a_bnd = jnp.zeros((2 * BND, SEG + WIDTH), F32)
    for k in range(4):
        row_at = 8.0 * chosen[:, k : k + 1] + chosen[:, 8 + k : 9 + k]
        a_bnd = a_bnd + jnp.where(at == row_at, chosen[:, 16 + k : 17 + k] + chosen[:, 24 + k : 25 + k], 0.0)
    a_bnd = a_bnd.astype(BF16)
    s[0:32, :] = picker[0:32]
    s[32:64, :] = a_bnd[0:32, 0:SEG]
    s[64:96, :] = picker[32:64]
    s[96:128, :] = a_bnd[32:64, 0:SEG]

    sends = []

    def exchange(n, src, dst, width, far_width):
        def move(j, there):
            first, size = (0, 64)[j % 2], (64, 32)[j // 2]
            base = (0, 64, 128, 160)[j]
            cols = slice(0, far_width if j >= 2 else width)
            return pltpu.make_async_remote_copy(
                src_ref=src.at[first : first + size, cols], dst_ref=dst.at[base : base + size, cols],
                send_sem=send_sem.at[n, j], recv_sem=recv_sem.at[n, j],
                device_id=there, device_id_type=MESH,
            )

        to_each(lambda j, there: move(j, there).start())
        moves = [move(j, {"dom": lax.rem(dom + 1, nd)}) for j in range(4)]
        sends.extend(enumerate(moves))
        return moves

    def received(moves, which):
        for j in which:
            pl.when(source[j])(moves[j].wait_recv)

    l_h0.wait()
    e0[:, 0:WIDTH] = dot(s[...], hb[...]).astype(BF16)
    e0[0:32, 2 * WIDTH :] = a_bnd[0:32, SEG:]
    e0[32:64, 2 * WIDTH :] = jnp.zeros((32, WIDTH), BF16)
    e0[64:96, 2 * WIDTH :] = a_bnd[32:64, SEG:]
    e0[96:128, 2 * WIDTH :] = jnp.zeros((32, WIDTH), BF16)
    l_x.wait()
    e0[:, WIDTH : 2 * WIDTH] = dot(s[...], x[:, 0:WIDTH]).astype(BF16)
    pl.semaphore_wait(barrier, guests + nr - 1)
    first = exchange(0, e0, r0, 3 * WIDTH, 2 * WIDTH)
    x_moves = []
    for part, (low, wide) in enumerate(((WIDTH, 2 * WIDTH), (3 * WIDTH, WIDTH))):
        ex[part, :, 0:wide] = dot(s[...], x[:, low : low + wide]).astype(BF16)
        x_moves.append(exchange(1 + part, ex.at[part], rx.at[part], wide, wide))

    rows, tall = jnp.transpose(near.astype(F32)), jnp.transpose(wts)
    step = 32
    lanes = iota((step, SEG + WIDTH), 1).astype(F32)
    for i in range(0, SEG, step):
        a = jnp.zeros((step, SEG + WIDTH), F32)
        for k in range(4):
            a = a + jnp.where(lanes == rows[i : i + step, k : k + 1], tall[i : i + step, k : k + 1], 0.0)
        a = a.astype(BF16)
        m[i : i + step, 0:SEG] = a[:, 0:SEG]
        ar[i : i + step, :] = a[:, SEG:]

    row, col = iota((WIDTH, 2 * WIDTH), 0), iota((WIDTH, 2 * WIDTH), 1)
    place = ((row < 32) & (col == row)) | ((row >= 32) & (row < 64) & (col == row + 32))
    m[0:SEG, SEG:] = dot(ar[...], place.astype(F32).astype(BF16)).astype(BF16)
    aa[...] = dot(m[0:SEG, 0:SEG], m[0:SEG, :])

    for c in l_path:
        c.wait()
    path = ip[...]
    path_hi, path_lo = lax.shift_right_logical(path, 7), path & (WIDTH - 1)
    which = (iota((SLOT_HI, ENT), 0) == path_hi).astype(F32).astype(BF16)
    slots = ps[...]
    slots_hi = lax.shift_right_logical(slots, 7).astype(F32).astype(BF16)
    slots_lo = (slots & (WIDTH - 1)).astype(F32).astype(BF16)
    at_lo = iota((WIDTH, ENT), 0) == path_lo
    contract0 = (((0,), (0,)), ((), ()))
    slot_hi = jnp.sum(
        jnp.where(at_lo, lax.dot_general(slots_hi, which, contract0, preferred_element_type=F32), 0.0),
        axis=0, keepdims=True,
    )
    slot_lo = jnp.sum(
        jnp.where(at_lo, lax.dot_general(slots_lo, which, contract0, preferred_element_type=F32), 0.0),
        axis=0, keepdims=True,
    )
    target = slot_hi * NBLK + ib[...].astype(F32)
    ones_lo = (iota((WIDTH, ENT), 0).astype(F32) == slot_lo).astype(F32).astype(BF16)
    for i in range(0, SLOT_HI * NBLK, 128):
        ones = (iota((128, ENT), 0).astype(F32) + float(i) == target).astype(F32).astype(BF16)
        count = lax.dot_general(ones, ones_lo, (((1,), (1,)), ((), ())), preferred_element_type=F32)
        top = count.astype(BF16)
        cnt[0, i : i + 128, :] = top
        cnt[1, i : i + 128, :] = (count - top.astype(F32)).astype(BF16)
    c_moves = []
    for k in range(1, nr):
        copy = pltpu.make_async_remote_copy(
            src_ref=cnt.at[:, pl.ds(pl.multiple_of(peers[k] * own_rows, own_rows), own_rows), :],
            dst_ref=crecv.at[k],
            send_sem=c_send.at[k], recv_sem=c_recv.at[k],
            device_id={"region": peers[k]}, device_id_type=MESH,
        )
        copy.start()
        c_moves.append(copy)
    crecv[0] = cnt[:, pl.ds(pl.multiple_of(region * own_rows, own_rows), own_rows), :]

    for c in l_w:
        c.wait()
    bias = jnp.concatenate([bg[...], bc[...]], axis=1)
    gx[0] = dot(x[:, 0:WIDTH], wx[0]) + bias

    received(first, range(4))
    lane = iota((32, WIDTH), 1)
    b_low, b_up = r0[0:32, 2 * WIDTH :].astype(F32), r0[64:96, 2 * WIDTH :].astype(F32)
    g_row, g_col = iota((32, WIDTH), 0), iota((32, WIDTH), 1)
    g[0:32, SEG : SEG + WIDTH] = (g_col == g_row + 32).astype(F32).astype(BF16)
    g[32:64, SEG : SEG + WIDTH] = (g_col == g_row + 96).astype(F32).astype(BF16)
    one_low, one_up = (lane == g_row + 64).astype(F32), (lane == g_row + 96).astype(F32)
    g[0:32, SEG + WIDTH :] = jnp.where(lane < 32, b_low, one_low).astype(BF16)
    g[32:64, SEG + WIDTH :] = jnp.where((lane >= 32) & (lane < 64), b_up, one_up).astype(BF16)
    back = jnp.concatenate(
        [jnp.where((lane >= 32) & (lane < 64), b_low, 0.0), jnp.where(lane < 32, b_up, 0.0)], axis=0
    ).astype(BF16)
    g[0:64, 0:SEG] = dot(back, pk[...]).astype(BF16)
    g[64:128, :] = jnp.zeros((64, SEG + 2 * WIDTH), BF16)
    m[SEG:, :] = (aa[...] + dot(ar[...], g[...])).astype(BF16)

    def x_spread(part):
        low, wide = (0, WIDTH, 3 * WIDTH)[part], (WIDTH, 2 * WIDTH, WIDTH)[part]
        if part:
            received(x_moves[part - 1], range(4))
        rows = rx[part - 1, :, 0:wide] if part else r0[:, WIDTH : 2 * WIDTH]
        both = (dot(m[:, 0:SEG], x[:, low : low + wide]) + dot(m[:, SEG:], rows)).astype(BF16)
        for i in range(wide // WIDTH):
            sx[low // WIDTH + i] = both[:, i * WIDTH : (i + 1) * WIDTH]

    def x_direct(t):
        gx[t] = dot(x[:, t * WIDTH : (t + 1) * WIDTH], wx[0]) + bias

    def x_project(t):
        gx[t] += dot(sx[t, 0:SEG], wx[1]) + dot(sx[t, SEG:], wx[2])

    def local(field, w):
        s12[:, 0:WIDTH] = dot(m[0:SEG, 0:SEG], field).astype(BF16)
        s12[:, WIDTH:] = dot(m[SEG:, 0:SEG], field).astype(BF16)
        return dot(field, w[0]) + dot(s12[...], w[1:3].reshape(2 * WIDTH, w.shape[2]))

    def remote(recv, w1, w2):
        bounds = jnp.concatenate([recv[0:32], recv[64:96]], axis=0)
        q = jnp.concatenate([dot(recv[0:192], w2), dot(bounds, w1)], axis=0).astype(BF16)
        return dot(m[SEG:, SEG:], q)

    def send_field(n, field):
        eh[n] = dot(s[...], field).astype(BF16)
        return exchange(3 + n, eh.at[n], rh.at[n], WIDTH, WIDTH)

    x_spread(0)
    x_project(0)
    h[...] = hb[...].astype(F32)
    moving, recv = None, r0.at[:, 0:WIDTH]
    for t in range(LAGS):
        pre[...] = gx[t, :, 0 : 2 * WIDTH] + local(hb[...], wgh)
        if t == 1:
            x_spread(2)
            x_direct(2)
        if t == 2:
            x_project(3)
        if t > 0:
            received(moving, range(4))
            recv = rh.at[2 * t - 1]
        reset = sigmoid(pre[:, 0:WIDTH] + remote(recv, wgh[1, :, 0:WIDTH], wgh[2, :, 0:WIDTH]))
        rhb[...] = (reset * h[...]).astype(BF16)
        moving = send_field(2 * t, rhb[...])
        upd[...] = sigmoid(pre[:, WIDTH:] + remote(recv, wgh[1, :, WIDTH:], wgh[2, :, WIDTH:]))
        pre[:, 0:WIDTH] = gx[t, :, 2 * WIDTH :] + local(rhb[...], wch)
        if t == 0:
            x_spread(1)
            x_direct(1)
            x_project(1)
        if t == 1:
            x_project(2)
            x_direct(3)
        received(moving, range(4))
        cand = jnp.tanh(pre[:, 0:WIDTH] + remote(rh.at[2 * t], wch[1], wch[2]))
        new = cand + upd[...] * (h[...] - cand)
        h[...] = new
        (hb if t < LAGS - 1 else sf_o)[...] = new.astype(BF16)
        if t < LAGS - 1:
            moving = send_field(2 * t + 1, hb[...])

    v = dot(sf_o[...], wo[...]) + bo[...]
    soft = jnp.maximum(v, 0.0) + jnp.log1p(jnp.exp(-jnp.abs(v)))
    block = 0.05 * jnp.sum(soft.reshape(NBLK, BS, WIDTH), axis=1)
    btsend[...] = block.astype(BF16)
    b_moves = []
    for k in sorted(range(1, nr), key=lambda k: abs(2 * k - nr)):
        copy = pltpu.make_async_remote_copy(
            src_ref=btsend, dst_ref=btrecv.at[k],
            send_sem=b_send.at[k], recv_sem=b_recv.at[k],
            device_id={"region": peers[k]}, device_id_type=MESH,
        )
        copy.start()
        b_moves.append(copy)
    btrecv[0] = btsend[...]
    for c in c_moves:
        c.wait_recv()
    for plane in range(2):
        for j in range(own_hi):
            part = crecv[:, plane, j * NBLK : (j + 1) * NBLK, :].reshape(nr * NBLK, WIDTH)
            ct[plane, j * WIDTH : (j + 1) * WIDTH, :] = jnp.transpose(part)
    for c in b_moves:
        c.wait_recv()
    times = btrecv[...].reshape(nr * NBLK, WIDTH)
    pt_o[...] = dot(ct[0], times) + dot(ct[1], times)
    for j, c in sends:
        pl.when(valid[j])(c.wait_send)
    for c in c_moves + b_moves:
        c.wait_send()


def solution(mesh):
    nr, nd = mesh.shape["region"], mesh.shape["dom"]
    owned = PATHS // nr
    own_rows = SLOT_HI // nr * NBLK
    vmem = pltpu.VMEM
    scratch = [
        vmem((8, SEG), jnp.int32), vmem((8, SEG), F32), vmem((1, 2 * BND), jnp.int32),
        vmem((SEG, LAGS * WIDTH), BF16),
        vmem((3, WIDTH, 3 * WIDTH), BF16), vmem((3, WIDTH, 2 * WIDTH), BF16), vmem((3, WIDTH, WIDTH), BF16),
        vmem((WIDTH, WIDTH), BF16),
        vmem((1, 2 * WIDTH), F32), vmem((1, WIDTH), F32), vmem((1, WIDTH), F32),
        vmem((1, ENT), jnp.int32), vmem((1, ENT), jnp.int32), vmem((SLOT_HI, WIDTH), jnp.int32),
        vmem((SEG, WIDTH), F32), vmem((SEG, WIDTH), BF16), vmem((SEG, WIDTH), BF16),
        vmem((2 * SEG, SEG + 2 * WIDTH), BF16), vmem((SEG, WIDTH), BF16), vmem((WIDTH, SEG), BF16),
        vmem((WIDTH, SEG), BF16), vmem((SEG, SEG + 2 * WIDTH), F32), vmem((WIDTH, SEG + 2 * WIDTH), BF16),
        vmem((SEG, 2 * WIDTH), BF16), vmem((LAGS, 2 * SEG, WIDTH), BF16),
        vmem((LAGS, SEG, 3 * WIDTH), F32), vmem((SEG, 2 * WIDTH), F32), vmem((SEG, WIDTH), F32),
        vmem((128, 3 * WIDTH), BF16), vmem((256, 3 * WIDTH), BF16),
        vmem((2, 128, 256), BF16), vmem((2, 256, 256), BF16),
        vmem((2 * LAGS - 1, 128, WIDTH), BF16), vmem((2 * LAGS - 1, 192, WIDTH), BF16),
        vmem((2, SLOT_HI * NBLK, WIDTH), BF16), vmem((nr, 2, own_rows, WIDTH), BF16),
        vmem((2, owned, nr * NBLK), BF16),
        vmem((NBLK, WIDTH), BF16), vmem((nr, NBLK, WIDTH), BF16),
        pltpu.SemaphoreType.DMA((16,)),
        pltpu.SemaphoreType.DMA((2 + 2 * LAGS, 4)), pltpu.SemaphoreType.DMA((2 + 2 * LAGS, 4)),
        pltpu.SemaphoreType.DMA((nr,)), pltpu.SemaphoreType.DMA((nr,)),
        pltpu.SemaphoreType.DMA((nr,)), pltpu.SemaphoreType.DMA((nr,)),
    ]
    call = pl.pallas_call(
        functools.partial(kernel, nr, nd),
        out_shape=(
            vmem((SEG, WIDTH), BF16),
            vmem((owned, WIDTH), F32),
        ),
        in_specs=[pl.BlockSpec(memory_space=pl.ANY)] * 14,
        out_specs=(pl.BlockSpec(memory_space=pltpu.VMEM), pl.BlockSpec(memory_space=pltpu.VMEM)),
        scratch_shapes=scratch,
        compiler_params=pltpu.CompilerParams(
            collective_id=0, has_side_effects=True, vmem_limit_bytes=56 * 1024 * 1024
        ),
        cost_estimate=pl.CostEstimate(flops=6 * 10**9, bytes_accessed=2 * 10**6, transcendentals=10**6),
    )

    def per_device(
        inputs, state_init, neighbors, edge_weight, boundary, w_gate, b_gate, w_cand, b_cand,
        w_out, b_out, inc_block, inc_path, path_slot,
    ):
        state, paths = call(
            jnp.transpose(neighbors), jnp.transpose(edge_weight), boundary.reshape(1, -1),
            state_init, inputs, w_gate, w_cand, w_out,
            b_gate.reshape(1, -1), b_cand.reshape(1, -1), b_out.reshape(1, -1),
            inc_block.reshape(1, -1), inc_path.reshape(1, -1), path_slot.reshape(SLOT_HI, WIDTH),
        )
        return state, paths[None]

    both = ("region", "dom")
    placed = (
        P(both, None), P(both, None), P(both, None), P(both, None), P(both),
        P(), P(), P(), P(), P(), P(), P(both), P(both), P("dom", None),
    )
    return jax.shard_map(
        per_device,
        mesh=mesh,
        in_specs=placed,
        out_specs=(P(both, None), P("dom", "region", None)),
        check_vma=False,
    )
```

```python
import functools

import jax
import jax.numpy as jnp
from jax import lax
from jax.experimental import pallas as pl
from jax.experimental.pallas import tpu as pltpu
from jax.sharding import PartitionSpec as P

MESH = pl.DeviceIdType.MESH
SEG, WIDTH, BND, NBLK, BS = 512, 128, 32, 32, 16
LAGS, ENT, PATHS = 4, 1024, 2048
SLOT_HI = PATHS // WIDTH
F32, BF16 = jnp.float32, jnp.bfloat16


def dot(a, b):
    return jnp.dot(a, b, preferred_element_type=F32)


def iota(shape, dim):
    return lax.broadcasted_iota(jnp.int32, shape, dim)


def sigmoid(v):
    return 0.5 * jnp.tanh(0.5 * v) + 0.5


def kernel(
    nr, nd,
    nbr_h, ew_h, bnd_h, h0_h, x_h, wg_h, wc_h, wo_h, bg_h, bc_h, bo_h, ib_h, ip_h, ps_h,
    sf_o, pt_o,
    nbr, ew, bnd, x, wx, wgh, wch, wo, bg, bc, bo, ib, ip, ps,
    h, hb, rhb, m, ar, pk, s, aa, g, s12, sx, gx, pre, upd,
    e0, r0, ex, rx, eh, rh,
    cnt, crecv, ct, btsend, btrecv,
    load_sem, send_sem, recv_sem, c_send, c_recv, b_send, b_recv,
):
    region, dom = lax.axis_index("region"), lax.axis_index("dom")
    hops = (1, -1, 2, -2)
    valid = [dom + hop < nd if hop > 0 else dom + hop >= 0 for hop in hops]
    source = [valid[1], valid[0], valid[3], valid[2]]
    guests = sum(v.astype(jnp.int32) for v in valid)

    def to_each(act, order=(2, 3, 0, 1)):
        for j in order:
            pl.when(valid[j])(functools.partial(act, j, {"dom": dom + hops[j]}))

    peers = [None] + [lax.rem(region + k, nr) for k in range(1, nr)]
    own_hi = SLOT_HI // nr
    own_rows = own_hi * NBLK

    loads = []

    def load(src, dst):
        copy = pltpu.make_async_copy(src, dst, load_sem.at[len(loads)])
        copy.start()
        loads.append(copy)
        return copy

    l_graph = [load(nbr_h, nbr.at[0:4]), load(ew_h, ew.at[0:4]), load(bnd_h, bnd)]
    l_h0 = load(h0_h, hb)
    l_x = load(x_h, x)
    l_path = [load(ib_h, ib), load(ip_h, ip), load(ps_h, ps)]
    l_w = [
        load(wg_h.at[:, 0:WIDTH, :], wx.at[:, :, 0 : 2 * WIDTH]),
        load(wc_h.at[:, 0:WIDTH, :], wx.at[:, :, 2 * WIDTH : 3 * WIDTH]),
        load(wg_h.at[:, WIDTH : 2 * WIDTH, :], wgh),
        load(wc_h.at[:, WIDTH : 2 * WIDTH, :], wch),
        load(bg_h, bg),
        load(bc_h, bc),
        load(wo_h, wo),
        load(bo_h, bo),
    ]

    r0[192:256, :] = jnp.zeros((64, 3 * WIDTH), BF16)
    rx[:, 192:256, :] = jnp.zeros((2, 64, 256), BF16)

    @pl.when((dom < 2) | (dom >= nd - 2))
    def _():
        r0[0:192, :] = jnp.zeros((192, 3 * WIDTH), BF16)
        rx[:, 0:192, :] = jnp.zeros((2, 192, 256), BF16)
        rh[...] = jnp.zeros((2 * LAGS - 1, 192, WIDTH), BF16)

    barrier = pltpu.get_barrier_semaphore()
    to_each(lambda j, there: pl.semaphore_signal(barrier, inc=1, device_id=there, device_id_type=MESH))
    for k in range(1, nr):
        pl.semaphore_signal(barrier, inc=1, device_id={"region": peers[k]}, device_id_type=MESH)

    for c in l_graph:
        c.wait()
    near = nbr[...]
    outside = ((dom == 0) & (near >= SEG) & (near < SEG + BND)) | (
        (dom == nd - 1) & (near >= SEG + BND)
    )
    near = jnp.where(outside, -1, near)
    wts = ew[...] / (ew[0:1, :] + ew[1:2, :] + ew[2:3, :] + ew[3:4, :])
    turn = lax.rem(iota((2 * BND, 2 * BND), 0) + BND, 2 * BND) == iota((2 * BND, 2 * BND), 1)
    picked = jnp.sum(jnp.where(turn, bnd[...].astype(F32), 0.0), axis=1, keepdims=True)
    picker = (iota((2 * BND, SEG), 1).astype(F32) == picked).astype(F32).astype(BF16)
    pk[0 : 2 * BND, :] = picker
    pk[2 * BND :, :] = jnp.zeros((2 * BND, SEG), BF16)
    w_top = wts.astype(BF16).astype(F32)
    edges = jnp.concatenate(
        [lax.shift_right_arithmetic(near, 3).astype(F32), (near & 7).astype(F32), w_top, wts - w_top], axis=0
    ).astype(BF16)
    chosen = lax.dot_general(picker, edges, (((1,), (1,)), ((), ())), preferred_element_type=F32)
    at = iota((2 * BND, SEG + WIDTH), 1).astype(F32)
    a_bnd = jnp.zeros((2 * BND, SEG + WIDTH), F32)
    for k in range(4):
        row_at = 8.0 * chosen[:, k : k + 1] + chosen[:, 8 + k : 9 + k]
        a_bnd = a_bnd + jnp.where(at == row_at, chosen[:, 16 + k : 17 + k] + chosen[:, 24 + k : 25 + k], 0.0)
    a_bnd = a_bnd.astype(BF16)
    s[0:32, :] = picker[0:32]
    s[32:64, :] = a_bnd[0:32, 0:SEG]
    s[64:96, :] = picker[32:64]
    s[96:128, :] = a_bnd[32:64, 0:SEG]

    sends = []

    def exchange(n, src, dst, width, far_width, between=None):
        def move(j, there):
            first, size = (0, 64)[j % 2], (64, 32)[j // 2]
            base = (0, 64, 128, 160)[j]
            cols = slice(0, far_width if j >= 2 else width)
            return pltpu.make_async_remote_copy(
                src_ref=src.at[first : first + size, cols], dst_ref=dst.at[base : base + size, cols],
                send_sem=send_sem.at[n, j], recv_sem=recv_sem.at[n, j],
                device_id=there, device_id_type=MESH,
            )

        to_each(lambda j, there: move(j, there).start(), (2, 3))
        if between is not None:
            between()
        to_each(lambda j, there: move(j, there).start(), (0, 1))
        moves = [move(j, {"dom": lax.rem(dom + 1, nd)}) for j in range(4)]
        sends.extend(enumerate(moves))
        return moves

    def received(moves, which):
        for j in which:
            pl.when(source[j])(moves[j].wait_recv)

    l_h0.wait()
    e0[:, 0:WIDTH] = dot(s[...], hb[...]).astype(BF16)
    e0[0:32, 2 * WIDTH :] = a_bnd[0:32, SEG:]
    e0[32:64, 2 * WIDTH :] = jnp.zeros((32, WIDTH), BF16)
    e0[64:96, 2 * WIDTH :] = a_bnd[32:64, SEG:]
    e0[96:128, 2 * WIDTH :] = jnp.zeros((32, WIDTH), BF16)
    l_x.wait()
    e0[:, WIDTH : 2 * WIDTH] = dot(s[...], x[:, 0:WIDTH]).astype(BF16)
    pl.semaphore_wait(barrier, guests + nr - 1)
    first = exchange(0, e0, r0, 3 * WIDTH, 2 * WIDTH)
    x_moves = []
    for part, (low, wide) in enumerate(((WIDTH, 2 * WIDTH), (3 * WIDTH, WIDTH))):
        ex[part, :, 0:wide] = dot(s[...], x[:, low : low + wide]).astype(BF16)
        x_moves.append(exchange(1 + part, ex.at[part], rx.at[part], wide, wide))

    rows, tall = jnp.transpose(near.astype(F32)), jnp.transpose(wts)
    step = 32
    lanes = iota((step, SEG + WIDTH), 1).astype(F32)
    for i in range(0, SEG, step):
        a = jnp.zeros((step, SEG + WIDTH), F32)
        for k in range(4):
            a = a + jnp.where(lanes == rows[i : i + step, k : k + 1], tall[i : i + step, k : k + 1], 0.0)
        a = a.astype(BF16)
        m[i : i + step, 0:SEG] = a[:, 0:SEG]
        ar[i : i + step, :] = a[:, SEG:]

    row, col = iota((WIDTH, 2 * WIDTH), 0), iota((WIDTH, 2 * WIDTH), 1)
    place = ((row < 32) & (col == row)) | ((row >= 32) & (row < 64) & (col == row + 32))
    m[0:SEG, SEG:] = dot(ar[...], place.astype(F32).astype(BF16)).astype(BF16)
    aa[...] = dot(m[0:SEG, 0:SEG], m[0:SEG, :])

    for c in l_path:
        c.wait()
    path = ip[...]
    path_hi, path_lo = lax.shift_right_logical(path, 7), path & (WIDTH - 1)
    which = (iota((SLOT_HI, ENT), 0) == path_hi).astype(F32).astype(BF16)
    slots = ps[...]
    slots_hi = lax.shift_right_logical(slots, 7).astype(F32).astype(BF16)
    slots_lo = (slots & (WIDTH - 1)).astype(F32).astype(BF16)
    at_lo = iota((WIDTH, ENT), 0) == path_lo
    contract0 = (((0,), (0,)), ((), ()))
    slot_hi = jnp.sum(
        jnp.where(at_lo, lax.dot_general(slots_hi, which, contract0, preferred_element_type=F32), 0.0),
        axis=0, keepdims=True,
    )
    slot_lo = jnp.sum(
        jnp.where(at_lo, lax.dot_general(slots_lo, which, contract0, preferred_element_type=F32), 0.0),
        axis=0, keepdims=True,
    )
    target = slot_hi * NBLK + ib[...].astype(F32)
    ones_lo = (iota((WIDTH, ENT), 0).astype(F32) == slot_lo).astype(F32).astype(BF16)
    for i in range(0, SLOT_HI * NBLK, 128):
        ones = (iota((128, ENT), 0).astype(F32) + float(i) == target).astype(F32).astype(BF16)
        count = lax.dot_general(ones, ones_lo, (((1,), (1,)), ((), ())), preferred_element_type=F32)
        top = count.astype(BF16)
        cnt[0, i : i + 128, :] = top
        cnt[1, i : i + 128, :] = (count - top.astype(F32)).astype(BF16)
    c_moves = []
    for k in range(1, nr):
        copy = pltpu.make_async_remote_copy(
            src_ref=cnt.at[:, pl.ds(pl.multiple_of(peers[k] * own_rows, own_rows), own_rows), :],
            dst_ref=crecv.at[k],
            send_sem=c_send.at[k], recv_sem=c_recv.at[k],
            device_id={"region": peers[k]}, device_id_type=MESH,
        )
        copy.start()
        c_moves.append(copy)
    crecv[0] = cnt[:, pl.ds(pl.multiple_of(region * own_rows, own_rows), own_rows), :]

    for c in l_w:
        c.wait()
    bias = jnp.concatenate([bg[...], bc[...]], axis=1)
    gx[0] = dot(x[:, 0:WIDTH], wx[0]) + bias

    received(first, range(4))
    lane = iota((32, WIDTH), 1)
    b_low, b_up = r0[0:32, 2 * WIDTH :].astype(F32), r0[64:96, 2 * WIDTH :].astype(F32)
    g_row, g_col = iota((32, WIDTH), 0), iota((32, WIDTH), 1)
    g[0:32, SEG : SEG + WIDTH] = (g_col == g_row + 32).astype(F32).astype(BF16)
    g[32:64, SEG : SEG + WIDTH] = (g_col == g_row + 96).astype(F32).astype(BF16)
    one_low, one_up = (lane == g_row + 64).astype(F32), (lane == g_row + 96).astype(F32)
    g[0:32, SEG + WIDTH :] = jnp.where(lane < 32, b_low, one_low).astype(BF16)
    g[32:64, SEG + WIDTH :] = jnp.where((lane >= 32) & (lane < 64), b_up, one_up).astype(BF16)
    back = jnp.concatenate(
        [jnp.where((lane >= 32) & (lane < 64), b_low, 0.0), jnp.where(lane < 32, b_up, 0.0)], axis=0
    ).astype(BF16)
    g[0:64, 0:SEG] = dot(back, pk[...]).astype(BF16)
    g[64:128, :] = jnp.zeros((64, SEG + 2 * WIDTH), BF16)
    m[SEG:, :] = (aa[...] + dot(ar[...], g[...])).astype(BF16)

    def x_spread(part):
        low, wide = (0, WIDTH, 3 * WIDTH)[part], (WIDTH, 2 * WIDTH, WIDTH)[part]
        if part:
            received(x_moves[part - 1], range(4))
        rows = rx[part - 1, :, 0:wide] if part else r0[:, WIDTH : 2 * WIDTH]
        both = (dot(m[:, 0:SEG], x[:, low : low + wide]) + dot(m[:, SEG:], rows)).astype(BF16)
        for i in range(wide // WIDTH):
            sx[low // WIDTH + i] = both[:, i * WIDTH : (i + 1) * WIDTH]

    def x_direct(t):
        gx[t] = dot(x[:, t * WIDTH : (t + 1) * WIDTH], wx[0]) + bias

    def x_project(t):
        gx[t] += dot(sx[t, 0:SEG], wx[1]) + dot(sx[t, SEG:], wx[2])

    def local(field, w):
        s12[:, 0:WIDTH] = dot(m[0:SEG, 0:SEG], field).astype(BF16)
        s12[:, WIDTH:] = dot(m[SEG:, 0:SEG], field).astype(BF16)
        return dot(field, w[0]) + dot(s12[...], w[1:3].reshape(2 * WIDTH, w.shape[2]))

    def remote(recv, w1, w2):
        bounds = jnp.concatenate([recv[0:32], recv[64:96]], axis=0)
        q = jnp.concatenate([dot(recv[0:192], w2), dot(bounds, w1)], axis=0).astype(BF16)
        return dot(m[SEG:, SEG:], q)

    def send_field(n, field):
        edge = dot(pk[0:64], field).astype(BF16)
        eh[n, 0:32], eh[n, 64:96] = edge[0:32], edge[32:64]

        def sums():
            part = dot(s[...], field).astype(BF16)
            eh[n, 32:64], eh[n, 96:128] = part[32:64], part[96:128]

        return exchange(3 + n, eh.at[n], rh.at[n], WIDTH, WIDTH, sums)

    x_spread(0)
    x_project(0)
    h[...] = hb[...].astype(F32)
    moving, recv = None, r0.at[:, 0:WIDTH]
    for t in range(LAGS):
        pre[...] = gx[t, :, 0 : 2 * WIDTH] + local(hb[...], wgh)
        if t == 1:
            x_spread(2)
            x_direct(2)
        if t == 2:
            x_project(3)
        if t > 0:
            received(moving, range(4))
            recv = rh.at[2 * t - 1]
        reset = sigmoid(pre[:, 0:WIDTH] + remote(recv, wgh[1, :, 0:WIDTH], wgh[2, :, 0:WIDTH]))
        rhb[...] = (reset * h[...]).astype(BF16)
        moving = send_field(2 * t, rhb[...])
        upd[...] = sigmoid(pre[:, WIDTH:] + remote(recv, wgh[1, :, WIDTH:], wgh[2, :, WIDTH:]))
        pre[:, 0:WIDTH] = gx[t, :, 2 * WIDTH :] + local(rhb[...], wch)
        if t == 0:
            x_spread(1)
            x_direct(1)
            x_project(1)
        if t == 1:
            x_project(2)
            x_direct(3)
        received(moving, range(4))
        cand = jnp.tanh(pre[:, 0:WIDTH] + remote(rh.at[2 * t], wch[1], wch[2]))
        new = cand + upd[...] * (h[...] - cand)
        h[...] = new
        (hb if t < LAGS - 1 else sf_o)[...] = new.astype(BF16)
        if t < LAGS - 1:
            moving = send_field(2 * t + 1, hb[...])

    v = dot(sf_o[...], wo[...]) + bo[...]
    soft = jnp.maximum(v, 0.0) + jnp.log1p(jnp.exp(-jnp.abs(v)))
    block = 0.05 * jnp.sum(soft.reshape(NBLK, BS, WIDTH), axis=1)
    btsend[...] = block.astype(BF16)
    b_moves = []
    for k in sorted(range(1, nr), key=lambda k: abs(2 * k - nr)):
        copy = pltpu.make_async_remote_copy(
            src_ref=btsend, dst_ref=btrecv.at[k],
            send_sem=b_send.at[k], recv_sem=b_recv.at[k],
            device_id={"region": peers[k]}, device_id_type=MESH,
        )
        copy.start()
        b_moves.append(copy)
    btrecv[0] = btsend[...]
    for c in c_moves:
        c.wait_recv()
    for plane in range(2):
        for j in range(own_hi):
            part = crecv[:, plane, j * NBLK : (j + 1) * NBLK, :].reshape(nr * NBLK, WIDTH)
            ct[plane, j * WIDTH : (j + 1) * WIDTH, :] = jnp.transpose(part)
    for j, c in sends:
        pl.when(valid[j])(c.wait_send)
    for c in c_moves + b_moves:
        c.wait_send()
    for c in b_moves:
        c.wait_recv()
    times = btrecv[...].reshape(nr * NBLK, WIDTH)
    pt_o[...] = dot(ct[0], times) + dot(ct[1], times)


def solution(mesh):
    nr, nd = mesh.shape["region"], mesh.shape["dom"]
    owned = PATHS // nr
    own_rows = SLOT_HI // nr * NBLK
    vmem = pltpu.VMEM
    scratch = [
        vmem((8, SEG), jnp.int32), vmem((8, SEG), F32), vmem((1, 2 * BND), jnp.int32),
        vmem((SEG, LAGS * WIDTH), BF16),
        vmem((3, WIDTH, 3 * WIDTH), BF16), vmem((3, WIDTH, 2 * WIDTH), BF16), vmem((3, WIDTH, WIDTH), BF16),
        vmem((WIDTH, WIDTH), BF16),
        vmem((1, 2 * WIDTH), F32), vmem((1, WIDTH), F32), vmem((1, WIDTH), F32),
        vmem((1, ENT), jnp.int32), vmem((1, ENT), jnp.int32), vmem((SLOT_HI, WIDTH), jnp.int32),
        vmem((SEG, WIDTH), F32), vmem((SEG, WIDTH), BF16), vmem((SEG, WIDTH), BF16),
        vmem((2 * SEG, SEG + 2 * WIDTH), BF16), vmem((SEG, WIDTH), BF16), vmem((WIDTH, SEG), BF16),
        vmem((WIDTH, SEG), BF16), vmem((SEG, SEG + 2 * WIDTH), F32), vmem((WIDTH, SEG + 2 * WIDTH), BF16),
        vmem((SEG, 2 * WIDTH), BF16), vmem((LAGS, 2 * SEG, WIDTH), BF16),
        vmem((LAGS, SEG, 3 * WIDTH), F32), vmem((SEG, 2 * WIDTH), F32), vmem((SEG, WIDTH), F32),
        vmem((128, 3 * WIDTH), BF16), vmem((256, 3 * WIDTH), BF16),
        vmem((2, 128, 256), BF16), vmem((2, 256, 256), BF16),
        vmem((2 * LAGS - 1, 128, WIDTH), BF16), vmem((2 * LAGS - 1, 192, WIDTH), BF16),
        vmem((2, SLOT_HI * NBLK, WIDTH), BF16), vmem((nr, 2, own_rows, WIDTH), BF16),
        vmem((2, owned, nr * NBLK), BF16),
        vmem((NBLK, WIDTH), BF16), vmem((nr, NBLK, WIDTH), BF16),
        pltpu.SemaphoreType.DMA((16,)),
        pltpu.SemaphoreType.DMA((2 + 2 * LAGS, 4)), pltpu.SemaphoreType.DMA((2 + 2 * LAGS, 4)),
        pltpu.SemaphoreType.DMA((nr,)), pltpu.SemaphoreType.DMA((nr,)),
        pltpu.SemaphoreType.DMA((nr,)), pltpu.SemaphoreType.DMA((nr,)),
    ]
    call = pl.pallas_call(
        functools.partial(kernel, nr, nd),
        out_shape=(
            vmem((SEG, WIDTH), BF16),
            vmem((owned, WIDTH), F32),
        ),
        in_specs=[pl.BlockSpec(memory_space=pl.ANY)] * 14,
        out_specs=(pl.BlockSpec(memory_space=pltpu.VMEM), pl.BlockSpec(memory_space=pltpu.VMEM)),
        scratch_shapes=scratch,
        compiler_params=pltpu.CompilerParams(
            collective_id=0, has_side_effects=True, vmem_limit_bytes=56 * 1024 * 1024
        ),
        cost_estimate=pl.CostEstimate(flops=6 * 10**9, bytes_accessed=2 * 10**6, transcendentals=10**6),
    )

    def per_device(
        inputs, state_init, neighbors, edge_weight, boundary, w_gate, b_gate, w_cand, b_cand,
        w_out, b_out, inc_block, inc_path, path_slot,
    ):
        state, paths = call(
            jnp.transpose(neighbors), jnp.transpose(edge_weight), boundary.reshape(1, -1),
            state_init, inputs, w_gate, w_cand, w_out,
            b_gate.reshape(1, -1), b_cand.reshape(1, -1), b_out.reshape(1, -1),
            inc_block.reshape(1, -1), inc_path.reshape(1, -1), path_slot.reshape(SLOT_HI, WIDTH),
        )
        return state, paths[None]

    both = ("region", "dom")
    placed = (
        P(both, None), P(both, None), P(both, None), P(both, None), P(both),
        P(), P(), P(), P(), P(), P(), P(both), P(both), P("dom", None),
    )
    return jax.shard_map(
        per_device,
        mesh=mesh,
        in_specs=placed,
        out_specs=(P(both, None), P("dom", "region", None)),
        check_vma=False,
    )
```
